256 devices in a mesh: wide: 32 (over z_hi, y, core), narrow: 8 (over x, z_lo).
Axes of the slice: x: 4, y: 4, z: 8 (z_hi: 4, z_lo: 2; z = z_hi * 2 + z_lo), core: 2. Of those that a mesh axis runs over, the one named last changes fastest.
Arguments:
- proj_a: bfloat16 [256, 32, 1024], P('narrow', None, 'wide'), may hold values from -12 to 12
- proj_b: bfloat16 [256, 32, 1024], P('wide', None, 'narrow'), may hold values from -12 to 12
- out_weight: bfloat16 [1024, 128], replicated, may hold values from -0.75 to 0.75
- out_bias: float32 [128], replicated, may hold values from -3 to 3
- pair_cotangent: bfloat16 [1024, 1024, 128], P('wide', 'narrow'), may hold values from -6 to 6
Outputs:
- pair_update: bfloat16 [1024, 1024, 128], P('wide', 'narrow')
- grad_a: bfloat16 [256, 32, 1024], P('narrow', None, 'wide')
- grad_b: bfloat16 [256, 32, 1024], P('wide', None, 'narrow')
The draws below stay inside these ranges and needn't reach their ends.
All inputs are finite; a program needn't handle non-finite values.
Results may differ from the reference program's by a relative error of at most 0.0049.
Values may be sent and summed in bfloat16 or wider, within the bound.
No kernel may reach another device: no remote copies, remote signals or barrier semaphores. Data moves between devices by JAX's collectives and lax.ppermute only.
A program may use at most 128 MiB of HBM per device.

```python
import math
import jax
import jax.numpy as jnp
from jax import lax

C = 32
OUT = 128
S = 256
R = 1024
CC = 1024


def steps_of(own_key, extent, split, low, top_value):
    loudness, own = 1.0, jax.random.fold_in(own_key, 6)
    for position, shards_of in split:
        draws = jnp.exp(jax.random.uniform(jax.random.fold_in(own, position), (shards_of,), jnp.float32, low / len(split), top_value / len(split)))
        loudness = loudness * jnp.repeat(draws, extent[position] // shards_of).reshape([-1 if axis == position else 1 for axis in range(len(extent))])
    return loudness


def centred(stream_key, shape, scale, most, cuts=(), kind=jnp.bfloat16):
    gain = steps_of(stream_key, shape, cuts, -0.22, 0.18) if cuts else 1.0
    result = jax.random.normal(stream_key, shape, jnp.float32) * scale * gain
    return jnp.minimum(jnp.maximum(result, -most), most).astype(kind)


def setup_inputs(seed: int = 0) -> dict:
    seeds = jax.random.split(jax.random.key(seed), 6)
    return {
        "proj_a": centred(seeds[0], (S, C, R), 2.0, 12.0, ((0, 8), (2, 32))),
        "proj_b": centred(seeds[1], (S, C, R), 2.0, 12.0, ((0, 32), (2, 8))),
        "out_weight": centred(seeds[2], (CC, OUT), (2 * C) ** -0.5, 0.75),
        "out_bias": centred(seeds[3], (OUT,), 0.5, 3.0, (), jnp.float32),
        "pair_cotangent": centred(seeds[4], (R, R, OUT), 1.0, 6.0, ((0, 32), (1, 8))),
    }


def reference(proj_a, proj_b, out_weight, out_bias, pair_cotangent):
    block = math.gcd(R, 64)
    count = R // block
    scale = 1.0 / S
    b_wide = proj_b.astype(jnp.float32)
    weight = out_weight.astype(jnp.float32)

    def one_block(carry, index):
        start = (index * block).astype(jnp.int32)
        a_rows = lax.dynamic_slice_in_dim(proj_a, start, block, 2).astype(jnp.float32)
        cot_rows = lax.dynamic_slice_in_dim(pair_cotangent, start, block, 0).astype(jnp.float32)
        outer = jnp.einsum("sci,sej->ijce", a_rows, b_wide) * scale
        outer = outer.astype(jnp.bfloat16).reshape(block, R, C * C).astype(jnp.float32)
        update = (jnp.einsum("ijf,fk->ijk", outer, weight) + out_bias).astype(jnp.bfloat16)
        grad_outer = jnp.einsum("ijk,fk->ijf", cot_rows, weight).astype(jnp.bfloat16)
        grad_outer = grad_outer.reshape(block, R, C, C).astype(jnp.float32)
        grad_rows = (jnp.einsum("ijce,sej->sci", grad_outer, b_wide) * scale).astype(jnp.bfloat16)
        carry = carry + jnp.einsum("ijce,sci->sej", grad_outer, a_rows)
        return carry, (update, grad_rows)

    start_total = jnp.zeros((S, C, R), jnp.float32)
    total, (updates, grad_blocks) = lax.scan(one_block, start_total, jnp.arange(count, dtype=jnp.int32))
    pair_update = updates.reshape(R, R, OUT)
    grad_a = jnp.transpose(grad_blocks, (1, 2, 0, 3)).reshape(S, C, R)
    grad_b = (total * scale).astype(jnp.bfloat16)
    return pair_update, grad_a, grad_b
```

```python
import functools

import jax
import jax.numpy as jnp
from jax import lax
from jax.experimental import pallas as pl
from jax.experimental.pallas import tpu as pltpu
from jax.sharding import PartitionSpec as P

F32 = jnp.float32
BF16 = jnp.bfloat16
C = 32
K = 128
SEQ = 256
ROWS = 32
COLS = 128
SCALE = 1.0 / SEQ
MIB = 1024 * 1024


def wide_perm(dz, dy, dc):
    perm = []
    for w in range(32):
        z, y, c = w // 8, (w // 2) % 4, w % 2
        perm.append((w, (((z + dz) % 4) * 4 + (y + dy) % 4) * 2 + (c ^ dc)))
    return perm


def narrow_perm(dx, dl):
    return [(n, ((n // 2 + dx) % 4) * 2 + ((n % 2) ^ dl)) for n in range(8)]


def send_z(v, k):
    return lax.ppermute(v, "wide", wide_perm(k, 0, 0))


def send_y(v, k):
    return lax.ppermute(v, "wide", wide_perm(0, k, 0))


def send_core(v):
    return lax.ppermute(v, "wide", wide_perm(0, 0, 1))


def send_x(v, k):
    return lax.ppermute(v, "narrow", narrow_perm(k, 0))


def send_l(v):
    return lax.ppermute(v, "narrow", narrow_perm(0, 1))


def own_row(place, rx, rl, yl, core):
    z, y, c, x, l = (place[q] for q in range(5))
    zz = lax.rem(x + rx - z + 8, 4)
    yy = lax.rem(2 * lax.rem(l + rl, 2) + yl - y + 8, 4)
    cc = lax.rem(core + c, 2)
    return pl.multiple_of(((cc * 4 + yy) * 4 + zz) * 8, 8)


def grad_outer_kernel(cot, w, g):
    count = cot.shape[0]
    both = cot[...].reshape(count * COLS, K)
    r = lax.dot_general(w[...], both, (((1,), (1,)), ((), ())), preferred_element_type=F32)
    r = r.astype(BF16)
    for i in range(count):
        for e in range(C):
            g[i * C:(i + 1) * C, e * COLS:(e + 1) * COLS] = r[e * C:(e + 1) * C, i * COLS:(i + 1) * COLS]


def grad_outer(cot, w):
    step = 4
    return pl.pallas_call(
        grad_outer_kernel,
        grid=(ROWS // step,),
        in_specs=[
            pl.BlockSpec((step, COLS, K), lambda r: (r, 0, 0)),
            pl.BlockSpec((C * C, K), lambda r: (0, 0)),
        ],
        out_specs=pl.BlockSpec((step * C, C * COLS), lambda r: (r, 0)),
        out_shape=jax.ShapeDtypeStruct((ROWS * C, C * COLS), BF16),
        compiler_params=pltpu.CompilerParams(vmem_limit_bytes=24 * MIB),
        cost_estimate=pl.CostEstimate(flops=2 * 4096 * 1024 * 128, bytes_accessed=9 * MIB, transcendentals=0),
        name="grad_outer",
    )(cot, w)


def grad_b_kernel(place, x0, x1, x2, x3, g, keep, away, at, order, a):
    @pl.when(pl.program_id(0) == 0)
    def _():
        for rx, piece in enumerate((x0, x1, x2, x3)):
            v = piece[...].astype(F32)
            for rl in range(2):
                for yl in range(2):
                    for core in range(2):
                        at_row = ((rl * 2 + yl) * 2 + core) * 8
                        order[pl.ds(own_row(place, rx, rl, yl, core), 8), :] = v[at_row:at_row + 8, :]
        v = order[...]
        a[...] = v.astype(BF16)
        at[...] = v.T.astype(BF16)

    r = jnp.dot(a[...], g[...], preferred_element_type=F32)
    keep[...] = r[:SEQ // 2]
    away[...] = r[SEQ // 2:].astype(BF16)


def grad_b_terms(place, xs, g):
    step = 512
    half = SEQ // 2
    piece = pl.BlockSpec((64, ROWS * C), lambda r: (0, 0))
    return pl.pallas_call(
        grad_b_kernel,
        grid=(C * COLS // step,),
        in_specs=[pl.BlockSpec(memory_space=pltpu.SMEM)] + [piece] * 4
        + [pl.BlockSpec((ROWS * C, step), lambda r: (0, r))],
        out_specs=[
            pl.BlockSpec((half, step), lambda r: (0, r)),
            pl.BlockSpec((half, step), lambda r: (0, r)),
            pl.BlockSpec((ROWS * C, SEQ), lambda r: (0, 0)),
        ],
        out_shape=[
            jax.ShapeDtypeStruct((half, C * COLS), F32),
            jax.ShapeDtypeStruct((half, C * COLS), BF16),
            jax.ShapeDtypeStruct((ROWS * C, SEQ), BF16),
        ],
        scratch_shapes=[pltpu.VMEM((SEQ, ROWS * C), F32), pltpu.VMEM((SEQ, ROWS * C), BF16)],
        compiler_params=pltpu.CompilerParams(vmem_limit_bytes=24 * MIB),
        cost_estimate=pl.CostEstimate(flops=2 * 4096 * 1024 * 256, bytes_accessed=12 * MIB, transcendentals=0),
        name="grad_b_terms",
    )(place, *xs, g)


def grad_a_kernel(place, b0, b1, b2, b3, b4, b5, b6, b7, g, keep, o1, o2, o3, b, r):
    @pl.when(pl.program_id(0) == 0)
    def _():
        for q, piece in enumerate((b0, b1, b2, b3, b4, b5, b6, b7)):
            b[q * 32:(q + 1) * 32, :] = piece[...]

    r[...] = lax.dot_general(b[...], g[...], (((1,), (1,)), ((), ())), preferred_element_type=F32)
    for rx, out in enumerate((keep, o1, o2, o3)):
        for rl in range(2):
            for yl in range(2):
                both = [r[pl.ds(own_row(place, rx, rl, yl, core), 8), :] for core in range(2)]
                row = (rl * 2 + yl) * 16
                out[row:row + 16, :] = jnp.concatenate(both, 0).astype(out.dtype)


def grad_a_terms(place, bs, g):
    step = 256
    piece = pl.BlockSpec((32, C * COLS), lambda r: (0, 0))
    out = pl.BlockSpec((64, step), lambda r: (0, r))
    return pl.pallas_call(
        grad_a_kernel,
        grid=(ROWS * C // step,),
        in_specs=[pl.BlockSpec(memory_space=pltpu.SMEM)] + [piece] * 8
        + [pl.BlockSpec((step, C * COLS), lambda r: (r, 0))],
        out_specs=[out] * 4,
        out_shape=[jax.ShapeDtypeStruct((64, ROWS * C), F32)]
        + [jax.ShapeDtypeStruct((64, ROWS * C), BF16)] * 3,
        scratch_shapes=[pltpu.VMEM((SEQ, C * COLS), BF16), pltpu.VMEM((SEQ, step), F32)],
        compiler_params=pltpu.CompilerParams(vmem_limit_bytes=24 * MIB),
        cost_estimate=pl.CostEstimate(flops=2 * 4096 * 1024 * 256, bytes_accessed=12 * MIB, transcendentals=0),
        name="grad_a_terms",
    )(place, *bs, g)


def update_kernel(at, b0, b1, b2, b3, b4, b5, b6, b7, wt, bias, out, b, o):
    @pl.when(pl.program_id(0) == 0)
    def _():
        for q, piece in enumerate((b0, b1, b2, b3, b4, b5, b6, b7)):
            b[q * 32:(q + 1) * 32, :] = piece[...]

    count = out.shape[0]
    wide = 8
    for start in range(0, C, wide):
        r = jnp.dot(at[...], b[:, start * COLS:(start + wide) * COLS], preferred_element_type=F32)
        r = (r * SCALE).astype(BF16)
        for i in range(count):
            for e in range(wide):
                row = (start + e) * C
                o[row:row + C, i * COLS:(i + 1) * COLS] = r[i * C:(i + 1) * C, e * COLS:(e + 1) * COLS]
    u = jnp.dot(wt[...], o[...], preferred_element_type=F32)
    for i in range(count):
        out[i] = (u[:, i * COLS:(i + 1) * COLS].T + bias[...]).astype(BF16)


def pair_update(at, bs, wt, bias):
    step = 8
    piece = pl.BlockSpec((32, C * COLS), lambda r: (0, 0))
    return pl.pallas_call(
        update_kernel,
        grid=(ROWS // step,),
        in_specs=[pl.BlockSpec((step * C, SEQ), lambda r: (r, 0))] + [piece] * 8
        + [pl.BlockSpec((K, C * C), lambda r: (0, 0)), pl.BlockSpec((1, K), lambda r: (0, 0))],
        out_specs=pl.BlockSpec((step, COLS, K), lambda r: (r, 0, 0)),
        out_shape=jax.ShapeDtypeStruct((ROWS, COLS, K), BF16),
        scratch_shapes=[pltpu.VMEM((SEQ, C * COLS), BF16), pltpu.VMEM((C * C, step * COLS), BF16)],
        compiler_params=pltpu.CompilerParams(vmem_limit_bytes=24 * MIB),
        cost_estimate=pl.CostEstimate(flops=3 * 4096 * 1024 * 256, bytes_accessed=4 * MIB, transcendentals=0),
        name="pair_update",
    )(at, *bs, wt, bias)


def shards(proj_a, proj_b, out_weight, out_bias, pair_cotangent):
    w = lax.axis_index("wide")
    n = lax.axis_index("narrow")
    place = jnp.stack([w // 8, (w // 2) % 4, w % 2, n // 2, n % 2]).astype(jnp.int32)

    a0 = proj_a.transpose(0, 2, 1).reshape(32, ROWS * C)
    a1 = send_l(a0)
    xs = [jnp.concatenate([a0, a1], 0)]
    xs += [send_x(xs[0], -k) for k in (1, 2, 3)]

    b0 = proj_b.reshape(8, C * COLS)
    zs = jnp.concatenate([b0] + [send_z(b0, -k) for k in (1, 2, 3)], 0)
    ys = [zs] + [send_y(zs, -k) for k in (1, 2, 3)]
    bs = ys + [send_core(v) for v in ys]

    weight = out_weight.reshape(C, C, K).transpose(1, 0, 2).reshape(C * C, K)
    g = grad_outer(pair_cotangent, weight)

    keep, away, at = grad_b_terms(place, xs, g)
    parts = {}
    for k in (2, 1, 3, 0):
        part = slice(32 * k, 32 * (k + 1))
        parts[k] = keep[part] + send_core(away[part]).astype(F32)
    total = parts[0]
    for k in (2, 1, 3):
        total = total + send_y(parts[k].astype(BF16), k).astype(F32)
    b_summed = total[:8]
    for k in (1, 2, 3):
        b_summed = b_summed + send_z(total[8 * k:8 * (k + 1)].astype(BF16), k).astype(F32)
    grad_b = (b_summed * SCALE).astype(BF16).reshape(8, C, COLS)

    kept, *others = grad_a_terms(place, bs, g)
    for k in (1, 2, 3):
        kept = kept + send_x(others[k - 1], k).astype(F32)
    a_summed = kept[:32] + send_l(kept[32:].astype(BF16)).astype(F32)
    grad_a = (a_summed * SCALE).astype(BF16).reshape(32, ROWS, C).transpose(0, 2, 1)

    update = pair_update(at, bs, weight.T, out_bias.reshape(1, K))
    return (update, grad_a, grad_b)


def solution(mesh):
    placed = (
        P("narrow", None, "wide"),
        P("wide", None, "narrow"),
        P(),
        P(),
        P("wide", "narrow", None),
    )
    return jax.shard_map(
        shards,
        mesh=mesh,
        in_specs=placed,
        out_specs=(P("wide", "narrow", None), P("narrow", None, "wide"), P("wide", None, "narrow")),
        check_vma=False,
    )
```

```python
import jax
import jax.numpy as jnp
from jax import lax
from jax.experimental import pallas as pl
from jax.experimental.pallas import tpu as pltpu
from jax.sharding import PartitionSpec as P

F32 = jnp.float32
BF16 = jnp.bfloat16
C = 32
K = 128
SEQ = 256
ROWS = 32
COLS = 128
SCALE = 1.0 / SEQ
MIB = 1024 * 1024


def wide_perm(dz, dy, dc):
    perm = []
    for w in range(32):
        z, y, c = w // 8, (w // 2) % 4, w % 2
        perm.append((w, ((z ^ dz) * 4 + (y + dy) % 4) * 2 + (c ^ dc)))
    return perm


def narrow_perm(dx, dl):
    return [(n, ((n // 2) ^ dx) * 2 + ((n % 2) ^ dl)) for n in range(8)]


def swap_z(v, d):
    return lax.ppermute(v, "wide", wide_perm(d, 0, 0))


def send_y(v, k):
    return lax.ppermute(v, "wide", wide_perm(0, k, 0))


def swap_core(v):
    return lax.ppermute(v, "wide", wide_perm(0, 0, 1))


def swap_x(v, d):
    return lax.ppermute(v, "narrow", narrow_perm(d, 0))


def swap_l(v):
    return lax.ppermute(v, "narrow", narrow_perm(0, 1))


def both(v, w):
    return jnp.concatenate([v, w], 0)


def own_row(place, qx, rl, yl, core):
    z, y, c, x, l = (place[q] for q in range(5))
    d = (x ^ (0, 1, 3, 2)[qx]) ^ z
    zz = d ^ (d >> 1)
    yy = lax.rem(2 * (l ^ rl) + yl - y + 4, 4)
    cc = core ^ c
    return pl.multiple_of(((cc * 4 + yy) * 4 + zz) * 8, 8)


def grad_outer_kernel(cot, w, g, wt, wide, wp):
    @pl.when(pl.program_id(0) == 0)
    def _():
        wide[...] = w[...].astype(F32)
        for e in range(C):
            wp[e * C:(e + 1) * C, :] = wide[pl.ds(e, C, stride=C), :].astype(BF16)
        wt[...] = wp[...].T

    count = cot.shape[0]
    rows = cot[...].reshape(count * COLS, K)
    r = lax.dot_general(wp[...], rows, (((1,), (1,)), ((), ())), preferred_element_type=F32)
    r = r.astype(BF16)
    for i in range(count):
        for e in range(C):
            g[pl.ds(pl.multiple_of((pl.program_id(0) * count + i) * C, C), C), e * COLS:(e + 1) * COLS] = r[e * C:(e + 1) * C, i * COLS:(i + 1) * COLS]


def grad_outer(cot, w):
    step = 32
    return pl.pallas_call(
        grad_outer_kernel,
        grid=(ROWS // step,),
        in_specs=[
            pl.BlockSpec((step, COLS, K), lambda r: (r, 0, 0)),
            pl.BlockSpec((C * C, K), lambda r: (0, 0)),
        ],
        out_specs=[
            pl.BlockSpec(memory_space=pltpu.VMEM),
            pl.BlockSpec((K, C * C), lambda r: (0, 0)),
        ],
        out_shape=[
            pltpu.VMEM((ROWS * C, C * COLS), BF16),
            jax.ShapeDtypeStruct((K, C * C), BF16),
        ],
        scratch_shapes=[pltpu.VMEM((C * C, K), F32), pltpu.VMEM((C * C, K), BF16)],
        compiler_params=pltpu.CompilerParams(vmem_limit_bytes=24 * MIB),
        cost_estimate=pl.CostEstimate(flops=2 * 4096 * 1024 * 128, bytes_accessed=9 * MIB, transcendentals=0),
        name="grad_outer",
    )(pltpu.with_memory_space_constraint(cot, pltpu.HBM), pltpu.with_memory_space_constraint(w, pltpu.HBM))


def grad_b_kernel(place, x0, x1, g, keep, away, at, order, a):
    if True:
        for qx in range(4):
            v = (x0, x1)[qx // 2][(qx % 2) * 64:(qx % 2 + 1) * 64, :].astype(F32)
            for rl in range(2):
                for yl in range(2):
                    for core in range(2):
                        at_row = ((rl * 2 + yl) * 2 + core) * 8
                        order[pl.ds(own_row(place, qx, rl, yl, core), 8), :] = v[at_row:at_row + 8, :]
        v = order[...]
        a[...] = v.astype(BF16)
        at[...] = v.T.astype(BF16)

    step = 4096

    def body(n, carry):
        cols = pl.ds(pl.multiple_of(n * step, step), step)
        r = jnp.dot(a[...], g[:, cols], preferred_element_type=F32)
        keep[:, cols] = r[:SEQ // 2]
        away[:, cols] = r[SEQ // 2:].astype(BF16)
        return carry

    lax.fori_loop(0, C * COLS // step, body, 0)


def grad_b_terms(place, xs, g):
    half = SEQ // 2
    whole = pl.BlockSpec(memory_space=pltpu.VMEM)
    return pl.pallas_call(
        grad_b_kernel,
        in_specs=[pl.BlockSpec(memory_space=pltpu.SMEM)] + [whole] * 3,
        out_specs=[whole] * 3,
        out_shape=[
            jax.ShapeDtypeStruct((half, C * COLS), F32),
            jax.ShapeDtypeStruct((half, C * COLS), BF16),
            jax.ShapeDtypeStruct((ROWS * C, SEQ), BF16),
        ],
        scratch_shapes=[pltpu.VMEM((SEQ, ROWS * C), F32), pltpu.VMEM((SEQ, ROWS * C), BF16)],
        compiler_params=pltpu.CompilerParams(vmem_limit_bytes=24 * MIB),
        cost_estimate=pl.CostEstimate(flops=2 * 4096 * 1024 * 256, bytes_accessed=12 * MIB, transcendentals=0),
        name="grad_b_terms",
    )(place, *xs, g)


def grad_a_kernel(place, b0, b1, b2, b3, b4, b5, b6, b7, g, keep, away, b, r):
    for q, piece in enumerate((b0, b1, b2, b3, b4, b5, b6, b7)):
        b[q * 32:(q + 1) * 32, :] = piece[...]
    step = 1024

    def body(n, carry):
        at = pl.ds(pl.multiple_of(n * step, step), step)
        r[...] = lax.dot_general(b[...], g[at, :], (((1,), (1,)), ((), ())), preferred_element_type=F32)
        for qx in range(4):
            out = (keep, away)[qx // 2]
            for rl in range(2):
                for yl in range(2):
                    pair = [r[pl.ds(own_row(place, qx, rl, yl, core), 8), :] for core in range(2)]
                    row = (qx % 2) * 64 + (rl * 2 + yl) * 16
                    out[row:row + 16, at] = jnp.concatenate(pair, 0).astype(out.dtype)
        return carry

    lax.fori_loop(0, ROWS * C // step, body, 0)


def grad_a_terms(place, bs, g):
    whole = pl.BlockSpec(memory_space=pltpu.VMEM)
    return pl.pallas_call(
        grad_a_kernel,
        in_specs=[pl.BlockSpec(memory_space=pltpu.SMEM)] + [whole] * 9,
        out_specs=[whole] * 3,
        out_shape=[
            jax.ShapeDtypeStruct((128, ROWS * C), F32),
            jax.ShapeDtypeStruct((128, ROWS * C), BF16),
            jax.ShapeDtypeStruct((SEQ, C * COLS), BF16),
        ],
        scratch_shapes=[pltpu.VMEM((SEQ, 1024), F32)],
        compiler_params=pltpu.CompilerParams(vmem_limit_bytes=24 * MIB),
        cost_estimate=pl.CostEstimate(flops=2 * 4096 * 1024 * 256, bytes_accessed=12 * MIB, transcendentals=0),
        name="grad_a_terms",
    )(place, *bs, g)


def update_kernel(at, b, wt, bias, out, o):
    count = out.shape[0]
    wide = 8
    for start in range(0, C, wide):
        r = jnp.dot(at[...], b[:, start * COLS:(start + wide) * COLS], preferred_element_type=F32)
        r = (r * SCALE).astype(BF16)
        for i in range(count):
            for e in range(wide):
                row = (start + e) * C
                o[row:row + C, i * COLS:(i + 1) * COLS] = r[i * C:(i + 1) * C, e * COLS:(e + 1) * COLS]
    u = jnp.dot(wt[...], o[...], preferred_element_type=F32)
    for i in range(count):
        out[i] = (u[:, i * COLS:(i + 1) * COLS].T + bias[...]).astype(BF16)


def pair_update(at, b, wt, bias):
    step = 32
    return pl.pallas_call(
        update_kernel,
        grid=(ROWS // step,),
        in_specs=[
            pl.BlockSpec((step * C, SEQ), lambda r: (r, 0)),
            pl.BlockSpec((SEQ, C * COLS), lambda r: (0, 0)),
            pl.BlockSpec((K, C * C), lambda r: (0, 0)),
            pl.BlockSpec((1, K), lambda r: (0, 0)),
        ],
        out_specs=pl.BlockSpec((step, COLS, K), lambda r: (r, 0, 0)),
        out_shape=jax.ShapeDtypeStruct((ROWS, COLS, K), BF16),
        scratch_shapes=[pltpu.VMEM((C * C, step * COLS), BF16)],
        compiler_params=pltpu.CompilerParams(vmem_limit_bytes=24 * MIB),
        cost_estimate=pl.CostEstimate(flops=3 * 4096 * 1024 * 256, bytes_accessed=4 * MIB, transcendentals=0),
        name="pair_update",
    )(at, b, wt, bias)


def shards(proj_a, proj_b, out_weight, out_bias, pair_cotangent):
    w = lax.axis_index("wide")
    n = lax.axis_index("narrow")
    place = jnp.stack([w >> 3, (w >> 1) & 3, w & 1, n >> 1, n & 1]).astype(jnp.int32)

    b0 = lax.optimization_barrier(proj_b.reshape(8, C * COLS))
    b1 = both(b0, swap_z(b0, 1))

    a0 = lax.optimization_barrier(proj_a.transpose(0, 2, 1).reshape(32, ROWS * C))
    a1 = both(a0, swap_l(a0))
    a2 = both(a1, swap_x(a1, 1))
    xs = [a2, swap_x(a2, 3)]

    b2 = both(b1, swap_z(b1, 3))
    ys = [b2] + [send_y(b2, -k) for k in (1, 2, 3)]
    bs = ys + [swap_core(v) for v in ys]

    place, pair_cotangent = lax.optimization_barrier((place, pair_cotangent))
    g, weight_t = grad_outer(pair_cotangent, out_weight)

    keep, away, at = grad_b_terms(place, xs, g)
    parts = {}
    for k in (2, 1, 3, 0):
        part = slice(32 * k, 32 * (k + 1))
        parts[k] = keep[part] + swap_core(away[part]).astype(F32)
    total = parts[0]
    for k in (2, 1, 3):
        total = total + send_y(parts[k].astype(BF16), k).astype(F32)
    b_summed = total[:8]
    for q, d in ((3, 2), (1, 1), (2, 3)):
        b_summed = b_summed + swap_z(total[8 * q:8 * (q + 1)].astype(BF16), d).astype(F32)
    grad_b = (b_summed * SCALE).astype(BF16).reshape(8, C, COLS)

    keep, away, b_full = grad_a_terms(place, bs, g)
    total = keep + swap_x(away, 3).astype(F32)
    total = total[:64] + swap_x(total[64:].astype(BF16), 1).astype(F32)
    a_summed = total[:32] + swap_l(total[32:].astype(BF16)).astype(F32)
    grad_a = (a_summed * SCALE).astype(BF16).reshape(32, ROWS, C).transpose(0, 2, 1)

    update = pair_update(at, b_full, weight_t, out_bias.reshape(1, K))
    return (update, grad_a, grad_b)


def solution(mesh):
    placed = (
        P("narrow", None, "wide"),
        P("wide", None, "narrow"),
        P(),
        P(),
        P("wide", "narrow", None),
    )
    return jax.shard_map(
        shards,
        mesh=mesh,
        in_specs=placed,
        out_specs=(P("wide", "narrow", None), P("narrow", None, "wide"), P("wide", None, "narrow")),
        check_vma=False,
    )
```

```python
import jax
import jax.numpy as jnp
from jax import lax
from jax.experimental import pallas as pl
from jax.experimental.pallas import tpu as pltpu
from jax.sharding import PartitionSpec as P

F32 = jnp.float32
BF16 = jnp.bfloat16
C = 32
K = 128
SEQ = 256
ROWS = 32
COLS = 128
SCALE = 1.0 / SEQ
MIB = 1024 * 1024


def wide_perm(dz, dy, dc):
    perm = []
    for w in range(32):
        z, y, c = w // 8, (w // 2) % 4, w % 2
        perm.append((w, ((z ^ dz[c]) * 4 + (y + dy) % 4) * 2 + (c ^ dc)))
    return perm


def narrow_perm(dl):
    return [(n, n ^ dl) for n in range(8)]


FIRST, SECOND = (1, 3), (3, 1)


def x_perm(d):
    perm = []
    for w in range(32):
        for n in range(8):
            perm.append((w * 8 + n, w * 8 + ((n // 2) ^ d[w % 2]) * 2 + n % 2))
    return perm


def swap_z(v, d):
    return lax.ppermute(v, "wide", wide_perm(d, 0, 0))


def send_y(v, k):
    return lax.ppermute(v, "wide", wide_perm((0, 0), k, 0))


def swap_core(v):
    return lax.ppermute(v, "wide", wide_perm((0, 0), 0, 1))


def swap_x(v, d):
    return lax.ppermute(v, ("wide", "narrow"), x_perm(d))


def swap_l(v):
    return lax.ppermute(v, "narrow", narrow_perm(1))


def both(v, w):
    return jnp.concatenate([v, w], 0)


def own_row(place, qx, rl, yl, core):
    z, y, c, x, l = (place[q] for q in range(5))
    on0, on1 = (0, 1, 3, 2)[qx], (0, 3, 1, 2)[qx]
    d = (x ^ (on0 + c * (on1 - on0))) ^ z
    d = d ^ ((d & 1) * 2 * core)
    zz = d ^ (d >> 1)
    yy = lax.rem(2 * (l ^ rl) + yl - y + 4, 4)
    cc = core ^ c
    return pl.multiple_of(((cc * 4 + yy) * 4 + zz) * 8, 8)


def grad_outer_kernel(cot, w, g, wt, wide, wp):
    @pl.when(pl.program_id(0) == 0)
    def _():
        wide[...] = w[...].astype(F32)
        for e in range(C):
            wp[e * C:(e + 1) * C, :] = wide[pl.ds(e, C, stride=C), :].astype(BF16)
        wt[...] = wp[...].T

    count = cot.shape[0]
    rows = cot[...].reshape(count * COLS, K)
    r = lax.dot_general(wp[...], rows, (((1,), (1,)), ((), ())), preferred_element_type=F32)
    r = r.astype(BF16)
    for i in range(count):
        for e in range(C):
            g[pl.ds(pl.multiple_of((pl.program_id(0) * count + i) * C, C), C), e * COLS:(e + 1) * COLS] = r[e * C:(e + 1) * C, i * COLS:(i + 1) * COLS]


def grad_outer(cot, w):
    step = 32
    return pl.pallas_call(
        grad_outer_kernel,
        grid=(ROWS // step,),
        in_specs=[
            pl.BlockSpec((step, COLS, K), lambda r: (r, 0, 0)),
            pl.BlockSpec((C * C, K), lambda r: (0, 0)),
        ],
        out_specs=[
            pl.BlockSpec(memory_space=pltpu.VMEM),
            pl.BlockSpec((K, C * C), lambda r: (0, 0)),
        ],
        out_shape=[
            pltpu.VMEM((ROWS * C, C * COLS), BF16),
            jax.ShapeDtypeStruct((K, C * C), BF16),
        ],
        scratch_shapes=[pltpu.VMEM((C * C, K), F32), pltpu.VMEM((C * C, K), BF16)],
        compiler_params=pltpu.CompilerParams(vmem_limit_bytes=24 * MIB),
        cost_estimate=pl.CostEstimate(flops=2 * 4096 * 1024 * 128, bytes_accessed=9 * MIB, transcendentals=0),
        name="grad_outer",
    )(pltpu.with_memory_space_constraint(cot, pltpu.HBM), pltpu.with_memory_space_constraint(w, pltpu.HBM))


def grad_b_kernel(place, x0, x1, g, keep, away, at, order, a):
    if True:
        for qx in range(4):
            v = (x0, x1)[qx // 2][(qx % 2) * 64:(qx % 2 + 1) * 64, :].astype(F32)
            for rl in range(2):
                for yl in range(2):
                    for core in range(2):
                        at_row = ((rl * 2 + yl) * 2 + core) * 8
                        order[pl.ds(own_row(place, qx, rl, yl, core), 8), :] = v[at_row:at_row + 8, :]
        v = order[...]
        a[...] = v.astype(BF16)
        at[...] = v.T.astype(BF16)

    step = 4096

    def body(n, carry):
        cols = pl.ds(pl.multiple_of(n * step, step), step)
        r = jnp.dot(a[...], g[:, cols], preferred_element_type=F32)
        keep[:, cols] = r[:SEQ // 2]
        away[:, cols] = r[SEQ // 2:].astype(BF16)
        return carry

    lax.fori_loop(0, C * COLS // step, body, 0)


def grad_b_terms(place, xs, g):
    half = SEQ // 2
    whole = pl.BlockSpec(memory_space=pltpu.VMEM)
    return pl.pallas_call(
        grad_b_kernel,
        in_specs=[pl.BlockSpec(memory_space=pltpu.SMEM)] + [whole] * 3,
        out_specs=[whole] * 3,
        out_shape=[
            jax.ShapeDtypeStruct((half, C * COLS), F32),
            jax.ShapeDtypeStruct((half, C * COLS), BF16),
            jax.ShapeDtypeStruct((ROWS * C, SEQ), BF16),
        ],
        scratch_shapes=[pltpu.VMEM((SEQ, ROWS * C), F32), pltpu.VMEM((SEQ, ROWS * C), BF16)],
        compiler_params=pltpu.CompilerParams(vmem_limit_bytes=24 * MIB),
        cost_estimate=pl.CostEstimate(flops=2 * 4096 * 1024 * 256, bytes_accessed=12 * MIB, transcendentals=0),
        name="grad_b_terms",
    )(place, *xs, g)


def grad_a_kernel(place, b0, b1, b2, b3, b4, b5, b6, b7, g, keep, away, b, r):
    for q, piece in enumerate((b0, b1, b2, b3, b4, b5, b6, b7)):
        b[q * 32:(q + 1) * 32, :] = piece[...]
    step = 1024

    def body(n, carry):
        at = pl.ds(pl.multiple_of(n * step, step), step)
        r[...] = lax.dot_general(b[...], g[at, :], (((1,), (1,)), ((), ())), preferred_element_type=F32)
        for qx in range(4):
            out = (keep, away)[qx // 2]
            for rl in range(2):
                for yl in range(2):
                    pair = [r[pl.ds(own_row(place, qx, rl, yl, core), 8), :] for core in range(2)]
                    row = (qx % 2) * 64 + (rl * 2 + yl) * 16
                    out[row:row + 16, at] = jnp.concatenate(pair, 0).astype(out.dtype)
        return carry

    lax.fori_loop(0, ROWS * C // step, body, 0)


def grad_a_terms(place, bs, g):
    whole = pl.BlockSpec(memory_space=pltpu.VMEM)
    return pl.pallas_call(
        grad_a_kernel,
        in_specs=[pl.BlockSpec(memory_space=pltpu.SMEM)] + [whole] * 9,
        out_specs=[whole] * 3,
        out_shape=[
            jax.ShapeDtypeStruct((128, ROWS * C), F32),
            jax.ShapeDtypeStruct((128, ROWS * C), BF16),
            jax.ShapeDtypeStruct((SEQ, C * COLS), BF16),
        ],
        scratch_shapes=[pltpu.VMEM((SEQ, 1024), F32)],
        compiler_params=pltpu.CompilerParams(vmem_limit_bytes=24 * MIB),
        cost_estimate=pl.CostEstimate(flops=2 * 4096 * 1024 * 256, bytes_accessed=12 * MIB, transcendentals=0),
        name="grad_a_terms",
    )(place, *bs, g)


def update_kernel(at, b, wt, bias, out, o):
    count = out.shape[0]
    wide = 8
    for start in range(0, C, wide):
        r = jnp.dot(at[...], b[:, start * COLS:(start + wide) * COLS], preferred_element_type=F32)
        r = (r * SCALE).astype(BF16)
        for i in range(count):
            for e in range(wide):
                row = (start + e) * C
                o[row:row + C, i * COLS:(i + 1) * COLS] = r[i * C:(i + 1) * C, e * COLS:(e + 1) * COLS]
    u = jnp.dot(wt[...], o[...], preferred_element_type=F32)
    for i in range(count):
        out[i] = (u[:, i * COLS:(i + 1) * COLS].T + bias[...]).astype(BF16)


def pair_update(at, b, wt, bias):
    step = 32
    return pl.pallas_call(
        update_kernel,
        grid=(ROWS // step,),
        in_specs=[
            pl.BlockSpec((step * C, SEQ), lambda r: (r, 0)),
            pl.BlockSpec((SEQ, C * COLS), lambda r: (0, 0)),
            pl.BlockSpec((K, C * C), lambda r: (0, 0)),
            pl.BlockSpec((1, K), lambda r: (0, 0)),
        ],
        out_specs=pl.BlockSpec((step, COLS, K), lambda r: (r, 0, 0)),
        out_shape=jax.ShapeDtypeStruct((ROWS, COLS, K), BF16),
        scratch_shapes=[pltpu.VMEM((C * C, step * COLS), BF16)],
        compiler_params=pltpu.CompilerParams(vmem_limit_bytes=24 * MIB),
        cost_estimate=pl.CostEstimate(flops=3 * 4096 * 1024 * 256, bytes_accessed=4 * MIB, transcendentals=0),
        name="pair_update",
    )(at, b, wt, bias)


def shards(proj_a, proj_b, out_weight, out_bias, pair_cotangent):
    w = lax.axis_index("wide")
    n = lax.axis_index("narrow")
    place = jnp.stack([w >> 3, (w >> 1) & 3, w & 1, n >> 1, n & 1]).astype(jnp.int32)

    b0 = lax.optimization_barrier(proj_b.reshape(8, C * COLS))
    b1 = both(b0, swap_z(b0, FIRST))

    a0 = lax.optimization_barrier(proj_a.transpose(0, 2, 1).reshape(32, ROWS * C))
    a1 = both(a0, swap_l(a0))
    a2 = both(a1, swap_x(a1, FIRST))
    xs = [a2, swap_x(a2, SECOND)]

    b2 = both(b1, swap_z(b1, SECOND))
    ys = [b2] + [send_y(b2, -k) for k in (1, 2, 3)]
    bs = ys + [swap_core(v) for v in ys]

    place, pair_cotangent = lax.optimization_barrier((place, pair_cotangent))
    g, weight_t = grad_outer(pair_cotangent, out_weight)

    keep, away, at = grad_b_terms(place, xs, g)
    parts = {}
    for k in (2, 1, 3, 0):
        part = slice(32 * k, 32 * (k + 1))
        parts[k] = keep[part] + swap_core(away[part]).astype(F32)
    total = parts[0]
    for k in (2, 1, 3):
        total = total + send_y(parts[k].astype(BF16), k).astype(F32)
    b_summed = total[:8]
    for q, d in ((3, (2, 2)), (1, FIRST), (2, SECOND)):
        b_summed = b_summed + swap_z(total[8 * q:8 * (q + 1)].astype(BF16), d).astype(F32)
    grad_b = (b_summed * SCALE).astype(BF16).reshape(8, C, COLS)

    keep, away, b_full = grad_a_terms(place, bs, g)
    total = keep + swap_x(away, SECOND).astype(F32)
    total = total[:64] + swap_x(total[64:].astype(BF16), FIRST).astype(F32)
    a_summed = total[:32] + swap_l(total[32:].astype(BF16)).astype(F32)
    grad_a = (a_summed * SCALE).astype(BF16).reshape(32, ROWS, C).transpose(0, 2, 1)

    update = pair_update(at, b_full, weight_t, out_bias.reshape(1, K))
    return (update, grad_a, grad_b)


def solution(mesh):
    placed = (
        P("narrow", None, "wide"),
        P("wide", None, "narrow"),
        P(),
        P(),
        P("wide", "narrow", None),
    )
    return jax.shard_map(
        shards,
        mesh=mesh,
        in_specs=placed,
        out_specs=(P("wide", "narrow", None), P("narrow", None, "wide"), P("wide", None, "narrow")),
        check_vma=False,
    )
```

```python
import jax
import jax.numpy as jnp
from jax import lax
from jax.experimental import pallas as pl
from jax.experimental.pallas import tpu as pltpu
from jax.sharding import PartitionSpec as P

F32 = jnp.float32
BF16 = jnp.bfloat16
C = 32
K = 128
SEQ = 256
ROWS = 32
COLS = 128
SCALE = 1.0 / SEQ
MIB = 1024 * 1024


def wide_perm(dz, dy, dc):
    perm = []
    for w in range(32):
        z, y, c = w // 8, (w // 2) % 4, w % 2
        perm.append((w, ((z ^ dz[c]) * 4 + (y + dy) % 4) * 2 + (c ^ dc)))
    return perm


def narrow_perm(dl):
    return [(n, n ^ dl) for n in range(8)]


FIRST, SECOND = (1, 3), (3, 1)


def x_perm(d):
    perm = []
    for w in range(32):
        for n in range(8):
            perm.append((w * 8 + n, w * 8 + ((n // 2) ^ d[w % 2]) * 2 + n % 2))
    return perm


def swap_z(v, d):
    return lax.ppermute(v, "wide", wide_perm(d, 0, 0))


def send_y(v, k):
    return lax.ppermute(v, "wide", wide_perm((0, 0), k, 0))


def swap_core(v):
    return lax.ppermute(v, "wide", wide_perm((0, 0), 0, 1))


def swap_x(v, d):
    return lax.ppermute(v, ("wide", "narrow"), x_perm(d))


def swap_l(v):
    return lax.ppermute(v, "narrow", narrow_perm(1))


def both(v, w):
    return jnp.concatenate([v, w], 0)


def own_row(place, qx, rl, yl, core):
    z, y, c, x, l = (place[q] for q in range(5))
    on0, on1 = (0, 1, 3, 2)[qx], (0, 3, 1, 2)[qx]
    d = (x ^ (on0 + c * (on1 - on0))) ^ z
    d = d ^ ((d & 1) * 2 * core)
    zz = d ^ (d >> 1)
    yy = lax.rem(2 * (l ^ rl) + yl - y + 4, 4)
    cc = core ^ c
    return pl.multiple_of(((cc * 4 + yy) * 4 + zz) * 8, 8)


def grad_outer_kernel(cot, w, g, wt, wide, wp):
    @pl.when(pl.program_id(0) == 0)
    def _():
        wide[...] = w[...].astype(F32)
        for e in range(C):
            wp[e * C:(e + 1) * C, :] = wide[pl.ds(e, C, stride=C), :].astype(BF16)
        wt[...] = wp[...].T

    count = cot.shape[0]
    rows = cot[...].reshape(count * COLS, K)
    r = lax.dot_general(wp[...], rows, (((1,), (1,)), ((), ())), preferred_element_type=F32)
    r = r.astype(BF16)
    for i in range(count):
        for e in range(C):
            g[pl.ds(pl.multiple_of((pl.program_id(0) * count + i) * C, C), C), e * COLS:(e + 1) * COLS] = r[e * C:(e + 1) * C, i * COLS:(i + 1) * COLS]


def grad_outer(cot, w):
    step = 32
    return pl.pallas_call(
        grad_outer_kernel,
        grid=(ROWS // step,),
        in_specs=[
            pl.BlockSpec((step, COLS, K), lambda r: (r, 0, 0)),
            pl.BlockSpec((C * C, K), lambda r: (0, 0)),
        ],
        out_specs=[
            pl.BlockSpec(memory_space=pltpu.VMEM),
            pl.BlockSpec((K, C * C), lambda r: (0, 0)),
        ],
        out_shape=[
            pltpu.VMEM((ROWS * C, C * COLS), BF16),
            jax.ShapeDtypeStruct((K, C * C), BF16),
        ],
        scratch_shapes=[pltpu.VMEM((C * C, K), F32), pltpu.VMEM((C * C, K), BF16)],
        compiler_params=pltpu.CompilerParams(vmem_limit_bytes=24 * MIB),
        cost_estimate=pl.CostEstimate(flops=2 * 4096 * 1024 * 128, bytes_accessed=9 * MIB, transcendentals=0),
        name="grad_outer",
    )(pltpu.with_memory_space_constraint(cot, pltpu.HBM), pltpu.with_memory_space_constraint(w, pltpu.HBM))


def grad_b_kernel(place, x0, x1, g, keep, away, at, order, a):
    if True:
        for qx in range(4):
            v = (x0, x1)[qx // 2][(qx % 2) * 64:(qx % 2 + 1) * 64, :].astype(F32)
            for rl in range(2):
                for yl in range(2):
                    for core in range(2):
                        at_row = ((rl * 2 + yl) * 2 + core) * 8
                        order[pl.ds(own_row(place, qx, rl, yl, core), 8), :] = v[at_row:at_row + 8, :]
        v = order[...]
        a[...] = v.astype(BF16)
        at[...] = v.T.astype(BF16)

    step = 4096

    def body(n, carry):
        cols = pl.ds(pl.multiple_of(n * step, step), step)
        r = jnp.dot(a[...], g[:, cols], preferred_element_type=F32)
        keep[:, cols] = r[:SEQ // 2]
        away[:, cols] = r[SEQ // 2:].astype(BF16)
        return carry

    lax.fori_loop(0, C * COLS // step, body, 0)


def grad_b_terms(place, xs, g):
    half = SEQ // 2
    whole = pl.BlockSpec(memory_space=pltpu.VMEM)
    return pl.pallas_call(
        grad_b_kernel,
        in_specs=[pl.BlockSpec(memory_space=pltpu.SMEM)] + [whole] * 3,
        out_specs=[whole] * 3,
        out_shape=[
            jax.ShapeDtypeStruct((half, C * COLS), F32),
            jax.ShapeDtypeStruct((half, C * COLS), BF16),
            jax.ShapeDtypeStruct((ROWS * C, SEQ), BF16),
        ],
        scratch_shapes=[pltpu.VMEM((SEQ, ROWS * C), F32), pltpu.VMEM((SEQ, ROWS * C), BF16)],
        compiler_params=pltpu.CompilerParams(vmem_limit_bytes=24 * MIB),
        cost_estimate=pl.CostEstimate(flops=2 * 4096 * 1024 * 256, bytes_accessed=12 * MIB, transcendentals=0),
        name="grad_b_terms",
    )(place, *xs, g)


def grad_a_kernel(place, b0, b1, b2, b3, b4, b5, b6, b7, g, keep, away, b, r):
    for q, piece in enumerate((b0, b1, b2, b3, b4, b5, b6, b7)):
        b[q * 32:(q + 1) * 32, :] = piece[...]
    step = 1024

    def body(n, carry):
        at = pl.ds(pl.multiple_of(n * step, step), step)
        r[...] = lax.dot_general(b[...], g[at, :], (((1,), (1,)), ((), ())), preferred_element_type=F32)
        for qx in range(4):
            out = (keep, away)[qx // 2]
            for rl in range(2):
                for yl in range(2):
                    pair = [r[pl.ds(own_row(place, qx, rl, yl, core), 8), :] for core in range(2)]
                    row = (qx % 2) * 64 + (rl * 2 + yl) * 16
                    out[row:row + 16, at] = jnp.concatenate(pair, 0).astype(out.dtype)
        return carry

    lax.fori_loop(0, ROWS * C // step, body, 0)


def grad_a_terms(place, bs, g):
    whole = pl.BlockSpec(memory_space=pltpu.VMEM)
    return pl.pallas_call(
        grad_a_kernel,
        in_specs=[pl.BlockSpec(memory_space=pltpu.SMEM)] + [whole] * 9,
        out_specs=[whole] * 3,
        out_shape=[
            jax.ShapeDtypeStruct((128, ROWS * C), F32),
            jax.ShapeDtypeStruct((128, ROWS * C), BF16),
            jax.ShapeDtypeStruct((SEQ, C * COLS), BF16),
        ],
        scratch_shapes=[pltpu.VMEM((SEQ, 1024), F32)],
        compiler_params=pltpu.CompilerParams(vmem_limit_bytes=24 * MIB),
        cost_estimate=pl.CostEstimate(flops=2 * 4096 * 1024 * 256, bytes_accessed=12 * MIB, transcendentals=0),
        name="grad_a_terms",
    )(place, *bs, g)


def update_kernel(at, b, wt, bias, out, o):
    count = out.shape[0]
    wide = 8
    for start in range(0, C, wide):
        r = jnp.dot(at[...], b[:, start * COLS:(start + wide) * COLS], preferred_element_type=F32)
        r = (r * SCALE).astype(BF16)
        for i in range(count):
            for e in range(wide):
                row = (start + e) * C
                o[row:row + C, i * COLS:(i + 1) * COLS] = r[i * C:(i + 1) * C, e * COLS:(e + 1) * COLS]
    u = jnp.dot(wt[...], o[...], preferred_element_type=F32)
    for i in range(count):
        out[i] = (u[:, i * COLS:(i + 1) * COLS].T + bias[...]).astype(BF16)


def pair_update(at, b, wt, bias):
    step = 32
    return pl.pallas_call(
        update_kernel,
        grid=(ROWS // step,),
        in_specs=[
            pl.BlockSpec((step * C, SEQ), lambda r: (r, 0)),
            pl.BlockSpec((SEQ, C * COLS), lambda r: (0, 0)),
            pl.BlockSpec((K, C * C), lambda r: (0, 0)),
            pl.BlockSpec((1, K), lambda r: (0, 0)),
        ],
        out_specs=pl.BlockSpec((step, COLS, K), lambda r: (r, 0, 0)),
        out_shape=jax.ShapeDtypeStruct((ROWS, COLS, K), BF16),
        scratch_shapes=[pltpu.VMEM((C * C, step * COLS), BF16)],
        compiler_params=pltpu.CompilerParams(vmem_limit_bytes=24 * MIB),
        cost_estimate=pl.CostEstimate(flops=3 * 4096 * 1024 * 256, bytes_accessed=4 * MIB, transcendentals=0),
        name="pair_update",
    )(at, b, wt, bias)


def shards(proj_a, proj_b, out_weight, out_bias, pair_cotangent):
    w = lax.axis_index("wide")
    n = lax.axis_index("narrow")
    place = jnp.stack([w >> 3, (w >> 1) & 3, w & 1, n >> 1, n & 1]).astype(jnp.int32)

    b0 = lax.optimization_barrier(proj_b.reshape(8, C * COLS))
    b1 = both(b0, swap_z(b0, FIRST))

    a0 = lax.optimization_barrier(proj_a.transpose(0, 2, 1).reshape(32, ROWS * C))
    a1 = both(a0, swap_l(a0))
    a2 = both(a1, swap_x(a1, FIRST))
    xs = [a2, swap_x(a2, SECOND)]

    b2 = both(b1, swap_z(b1, SECOND))
    ys = [b2] + [send_y(b2, -k) for k in (1, 2, 3)]
    bs = ys + [swap_core(v) for v in ys]

    place, pair_cotangent = lax.optimization_barrier((place, pair_cotangent))
    g, weight_t = grad_outer(pair_cotangent, out_weight)

    keep, away, at = grad_b_terms(place, xs, g)
    parts = {}
    for k in (2, 1, 3, 0):
        part = slice(32 * k, 32 * (k + 1))
        parts[k] = keep[part] + swap_core(away[part]).astype(F32)
    total = parts[0]
    for k in (2, 1, 3):
        total = total + send_y(parts[k].astype(BF16), k).astype(F32)
    b_summed = total[:8]
    for q, d in ((3, (2, 2)), (2, SECOND), (1, FIRST)):
        b_summed = b_summed + swap_z(total[8 * q:8 * (q + 1)].astype(BF16), d).astype(F32)
    grad_b = (b_summed * SCALE).astype(BF16).reshape(8, C, COLS)

    keep, away, b_full = grad_a_terms(place, bs, g)
    total = keep + swap_x(away, SECOND).astype(F32)
    total = total[:64] + swap_x(total[64:].astype(BF16), FIRST).astype(F32)
    a_summed = total[:32] + swap_l(total[32:].astype(BF16)).astype(F32)
    grad_a = (a_summed * SCALE).astype(BF16).reshape(32, ROWS, C).transpose(0, 2, 1)

    update = pair_update(at, b_full, weight_t, out_bias.reshape(1, K))
    return (update, grad_a, grad_b)


def solution(mesh):
    placed = (
        P("narrow", None, "wide"),
        P("wide", None, "narrow"),
        P(),
        P(),
        P("wide", "narrow", None),
    )
    return jax.shard_map(
        shards,
        mesh=mesh,
        in_specs=placed,
        out_specs=(P("wide", "narrow", None), P("narrow", None, "wide"), P("wide", None, "narrow")),
        check_vma=False,
    )
```
